1024 devices in a mesh: blk: 128 (over x, y, z_lo), lap: 8 (over z_hi, core).
Axes of the slice: x: 8, y: 8, z: 8 (z_hi: 4, z_lo: 2; z = z_hi * 2 + z_lo), core: 2. Of those that a mesh axis runs over, the one named last changes fastest.
Arguments:
- picture_encodings: bfloat16 [262144, 1152], P(('blk', 'lap')), may hold values from -0.1875 to 0.1875
- sentence_encodings: bfloat16 [262144, 1152], P(('blk', 'lap')), may hold values from -0.1875 to 0.1875
- sharpness_factor: float32 [1], replicated, may hold values from 4 to 8
- additive_shift_term: float32 [1], replicated, may hold values from -3 to -1
Outputs:
- per_row_loss: float32 [262144], P(('blk', 'lap'))
- picture_derivative_matrix: float32 [262144, 1152], P(('blk', 'lap'))
- grad_text: float32 [262144, 1152], P(('blk', 'lap'))
The draws below stay inside these ranges and needn't reach their ends.
All inputs are finite; a program needn't handle non-finite values.
Results may differ from the reference program's by a relative error of at most 0.003.
Values may be sent and summed in bfloat16 or wider, within the bound.
No kernel may reach another device: no remote copies, remote signals or barrier semaphores. Data moves between devices by JAX's collectives and lax.ppermute only.
A program may use at most 32 MiB of HBM per device.

```python
import jax
import jax.numpy as jnp

D = 1152
ROWS = 256
STEPS = 4
PAIRS = 262144
N_BLK = 128
N_LAP = 8


def level_of(rng, dims, split, smallest, high):
    def one(axis_at, shards_of):
        draws = jax.random.uniform(jax.random.fold_in(jax.random.fold_in(rng, 6), axis_at), (shards_of,), jnp.float32, smallest / len(split), high / len(split))
        return jnp.repeat(jnp.exp(draws), dims[axis_at] // shards_of).reshape((-1,) + (1,) * (len(dims) - axis_at - 1))

    factor_of = one(*split[0])
    for cut in split[1:]:
        factor_of = factor_of * one(*cut)
    return factor_of


def normal_values(stream_key, dims, spread, most, pieces=(), held_as=jnp.bfloat16):
    level = level_of(stream_key, dims, pieces, -0.22, 0.18) if pieces else 1.0
    result = jax.random.normal(stream_key, dims, jnp.float32) * spread * level
    return jnp.minimum(jnp.maximum(result, -most), most).astype(held_as)


def setup_inputs(seed: int = 0) -> dict:
    seeds = jax.random.split(jax.random.key(seed), 5)
    return {
        "picture_encodings": normal_values(seeds[0], (PAIRS, D), D ** -0.5, 0.1875, ((0, 1024),)),
        "sentence_encodings": normal_values(seeds[1], (PAIRS, D), D ** -0.5, 0.1875, ((0, 1024),)),
        "sharpness_factor": jnp.clip(jax.random.uniform(seeds[2], (1,), jnp.float32, 4.0, 8.0), 4.0, 8.0),
        "additive_shift_term": jnp.clip(jax.random.uniform(seeds[3], (1,), jnp.float32, -3.0, -1.0), -3.0, -1.0),
    }


def reference(picture_encodings, sentence_encodings, sharpness_factor, additive_shift_term):
    multiplier_factor = sharpness_factor[0]
    bias = additive_shift_term[0]
    blocks = N_BLK * N_LAP
    image_vectors32 = picture_encodings.reshape(blocks, ROWS, D).astype(jnp.float32)
    texts = sentence_encodings.reshape(blocks, ROWS, D)
    matched_entries = jnp.eye(ROWS, dtype=jnp.bool_)
    loss_sum = jnp.zeros((blocks, ROWS), jnp.float32)
    grad_img = jnp.zeros((blocks, ROWS, D), jnp.float32)
    sentence_derivative_matrix = jnp.zeros((blocks, ROWS, D), jnp.float32)
    for step in range(STEPS):
        paired32 = jnp.roll(texts, step, axis=0).astype(jnp.float32)
        inner = jnp.einsum("qrd,qsd->qrs", image_vectors32, paired32)
        logits = multiplier_factor * inner + bias
        if step == 0:
            label = jnp.where(matched_entries, 1.0, -1.0).astype(jnp.float32)
        else:
            label = jnp.full((ROWS, ROWS), -1.0, jnp.float32)
        loss_sum = loss_sum + jnp.sum(jax.nn.softplus(-label * logits), axis=2)
        weight = (multiplier_factor * (-label) * jax.nn.sigmoid(-label * logits)).astype(jnp.bfloat16)
        weight32 = weight.astype(jnp.float32)
        grad_img = grad_img + jnp.einsum("qrs,qsd->qrd", weight32, paired32)
        contrib = jnp.einsum("qrs,qrd->qsd", weight32, image_vectors32)
        sentence_derivative_matrix = sentence_derivative_matrix + jnp.roll(contrib, -step, axis=0)
    per_row_loss = (loss_sum / (STEPS * ROWS)).reshape(blocks * ROWS)
    return per_row_loss, grad_img.reshape(blocks * ROWS, D), sentence_derivative_matrix.reshape(blocks * ROWS, D)
```

```python
import jax
import jax.numpy as jnp
from jax import lax
from jax.sharding import PartitionSpec as P

STEPS = 4
AXES = ("blk", "lap")


def swap(block, between_chips):
    count = lax.axis_size(AXES)
    other = 1 if between_chips else 0
    route = [(i, (i + 1 if i % 2 == other else i - 1) % count) for i in range(count)]
    return lax.ppermute(block, AXES, route)


def logits_of(own, arrived, scale, bias):
    inner = lax.dot_general(own, arrived, (((1,), (1,)), ((), ())), preferred_element_type=jnp.float32)
    return scale * inner + bias


def unmatched(own, arrived, scale, bias):
    logits = logits_of(own, arrived, scale, bias)
    losses = jnp.sum(jax.nn.softplus(logits), axis=1)
    weight = (scale * jax.nn.sigmoid(logits)).astype(jnp.bfloat16)
    return losses, jnp.dot(weight, arrived, preferred_element_type=jnp.float32)


def per_device(picture_encodings, sentence_encodings, sharpness_factor, additive_shift_term):
    scale = sharpness_factor[0]
    bias = additive_shift_term[0]
    count = picture_encodings.shape[0]
    even = lax.axis_index("lap") % 2 == 0
    outer = jnp.where(even, picture_encodings, sentence_encodings)
    inner = jnp.where(even, sentence_encodings, picture_encodings)

    outer_1 = swap(outer, True)
    inner_1 = swap(inner, False)
    outer_2 = swap(inner_1, True)
    inner_2 = swap(outer_1, False)
    outer_3 = swap(inner_2, True)
    inner_3 = swap(outer_2, False)

    logits = logits_of(outer, inner, scale, bias)
    label = jnp.where(jnp.eye(count, dtype=jnp.bool_), 1.0, -1.0).astype(jnp.float32)
    losses = jax.nn.softplus(-label * logits)
    weight = (scale * -label * jax.nn.sigmoid(-label * logits)).astype(jnp.bfloat16)
    outer_loss = jnp.sum(losses, axis=1)
    inner_loss = jnp.sum(losses, axis=0)
    outer_grad = jnp.dot(weight, inner, preferred_element_type=jnp.float32)
    inner_grad = lax.dot_general(weight, outer, (((0,), (0,)), ((), ())), preferred_element_type=jnp.float32)
    for arrived in (inner_1, inner_2, inner_3):
        loss, grad = unmatched(inner, arrived, scale, bias)
        inner_loss = inner_loss + loss
        inner_grad = inner_grad + grad
    for arrived in (outer_1, outer_2, outer_3):
        loss, grad = unmatched(outer, arrived, scale, bias)
        outer_loss = outer_loss + loss
        outer_grad = outer_grad + grad
    per_row_loss = jnp.where(even, outer_loss, inner_loss) / (STEPS * count)
    return (
        per_row_loss,
        jnp.where(even, outer_grad, inner_grad),
        jnp.where(even, inner_grad, outer_grad),
    )


def solution(mesh):
    placed = (P(AXES, None), P(AXES, None), P(), P())
    return jax.shard_map(
        per_device,
        mesh=mesh,
        in_specs=placed,
        out_specs=(P(AXES), P(AXES, None), P(AXES, None)),
        check_vma=False,
    )
```

```python
import jax
import jax.numpy as jnp
from jax import lax
from jax.sharding import PartitionSpec as P

STEPS = 4
AXES = ("blk", "lap")


def moved(block, even_by, odd_by):
    count = lax.axis_size(AXES)
    route = [(i, (i + (odd_by if i % 2 else even_by)) % count) for i in range(count)]
    return lax.ppermute(block, AXES, route)


def logits_of(own, arrived, scale, bias):
    inner = lax.dot_general(own, arrived, (((1,), (1,)), ((), ())), preferred_element_type=jnp.float32)
    return scale * inner + bias


def unmatched(own, arrived, scale, bias):
    logits = logits_of(own, arrived, scale, bias)
    losses = jnp.sum(jax.nn.softplus(logits), axis=1)
    weight = (scale * jax.nn.sigmoid(logits)).astype(jnp.bfloat16)
    return losses, jnp.dot(weight, arrived, preferred_element_type=jnp.float32)


def per_device(picture_encodings, sentence_encodings, sharpness_factor, additive_shift_term):
    scale = sharpness_factor[0]
    bias = additive_shift_term[0]
    count = picture_encodings.shape[0]
    even = lax.axis_index("lap") % 2 == 0
    outer = jnp.where(even, picture_encodings, sentence_encodings)
    inner = jnp.where(even, sentence_encodings, picture_encodings)

    outer_1 = moved(outer, -1, 1)
    inner_3 = moved(inner, 3, -3)
    inner_1 = moved(inner, 1, -1)
    outer_3 = moved(outer_1, 2, -2)
    inner_2 = moved(outer_1, 1, -1)
    outer_2 = moved(inner_3, 1, -1)

    outer_own, inner_own, _ = lax.optimization_barrier((outer, inner, outer_1))
    logits = logits_of(outer_own, inner_own, scale, bias)
    label = jnp.where(jnp.eye(count, dtype=jnp.bool_), 1.0, -1.0).astype(jnp.float32)
    losses = jax.nn.softplus(-label * logits)
    weight = (scale * -label * jax.nn.sigmoid(-label * logits)).astype(jnp.bfloat16)
    outer_loss = jnp.sum(losses, axis=1)
    inner_loss = jnp.sum(losses, axis=0)
    outer_grad = jnp.dot(weight, inner_own, preferred_element_type=jnp.float32)
    inner_grad = lax.dot_general(weight, outer_own, (((0,), (0,)), ((), ())), preferred_element_type=jnp.float32)
    for arrived in (inner_1, inner_2, inner_3):
        loss, grad = unmatched(inner, arrived, scale, bias)
        inner_loss = inner_loss + loss
        inner_grad = inner_grad + grad
    for arrived in (outer_1, outer_2):
        loss, grad = unmatched(outer, arrived, scale, bias)
        outer_loss = outer_loss + loss
        outer_grad = outer_grad + grad
    outer_3, outer_loss, outer_grad, inner_loss, inner_grad = lax.optimization_barrier(
        (outer_3, outer_loss, outer_grad, inner_loss, inner_grad)
    )
    loss, grad = unmatched(outer, outer_3, scale, bias)
    outer_loss = outer_loss + loss
    outer_grad = outer_grad + grad
    per_row_loss = jnp.where(even, outer_loss, inner_loss) / (STEPS * count)
    return (
        per_row_loss,
        jnp.where(even, outer_grad, inner_grad),
        jnp.where(even, inner_grad, outer_grad),
    )


def solution(mesh):
    placed = (P(AXES, None), P(AXES, None), P(), P())
    return jax.shard_map(
        per_device,
        mesh=mesh,
        in_specs=placed,
        out_specs=(P(AXES), P(AXES, None), P(AXES, None)),
        check_vma=False,
    )
```

```python
import jax
import jax.numpy as jnp
from jax import lax
from jax.experimental import pallas as pl
from jax.experimental.pallas import tpu as pltpu
from jax.sharding import PartitionSpec as P

STEPS = 4
AXES = ("blk", "lap")
PARTS = 3
SMEM = pl.BlockSpec(memory_space=pltpu.SMEM)
VMEM = pl.BlockSpec(memory_space=pltpu.VMEM)
ANY = pl.BlockSpec(memory_space=pl.ANY)


def moved(block, even_by, odd_by, sends=lambda i: True):
    count = lax.axis_size(AXES)
    route = [(i, (i + (odd_by if i % 2 else even_by)) % count) for i in range(count) if sends(i)]
    return lax.ppermute(block, AXES, route)


def after(block, *earlier):
    return lax.optimization_barrier((block, *earlier))[0]


def logits_of(own, arrived, scale, bias):
    inner = lax.dot_general(own, arrived, (((1,), (1,)), ((), ())), preferred_element_type=jnp.float32)
    return scale * inner + bias


def sigmoid_parts(logits):
    small = jnp.exp(-jnp.abs(logits))
    return small, jnp.where(logits >= 0.0, 1.0, small) / (1.0 + small)


def times(weight, block):
    return jnp.dot(weight, block, preferred_element_type=jnp.float32)


def add_losses(logits, small, linear, product):
    linear[...] += jnp.maximum(logits, 0.0)
    product[...] += small + product[...] * small


def add_tile(scale, bias, own, arrived, grad, linear, product, has_losses):
    logits = logits_of(own[...], arrived[...], scale, bias)
    small, sigmoid = sigmoid_parts(logits)
    grad[...] += times((scale * sigmoid).astype(jnp.bfloat16), arrived[...])

    @pl.when(has_losses)
    def _():
        add_losses(logits, small, linear, product)


def own_tile(
    even_ref, straight_ref, scale_ref, bias_ref, outer, inner, straight, outer_grad, inner_grad, linear, product
):
    scale, bias = scale_ref[0], bias_ref[0]
    even = even_ref[0] == 1
    count = outer.shape[0]
    logits = logits_of(outer[...], inner[...], scale, bias)
    matched = lax.broadcasted_iota(jnp.int32, (count, count), 0) == lax.broadcasted_iota(jnp.int32, (count, count), 1)
    sign = jnp.where(matched, -1.0, 1.0)
    logits = sign * logits
    small, sigmoid = sigmoid_parts(logits)
    weight = (scale * sign * sigmoid).astype(jnp.bfloat16)
    outer_grad[...] = times(weight, inner[...])
    inner_grad[...] = lax.dot_general(weight, outer[...], (((0,), (0,)), ((), ())), preferred_element_type=jnp.float32)

    @pl.when(even)
    def _():
        linear[...] = jnp.maximum(logits, 0.0)
        product[...] = small

    @pl.when(jnp.logical_not(even))
    def _():
        linear[...] = jnp.maximum(logits, 0.0).T
        product[...] = small.T

    @pl.when(straight_ref[0] == 1)
    def _():
        add_tile(scale, bias, outer, straight, outer_grad, linear, product, even)


def first_tiles(
    even_ref, scale_ref, bias_ref, outer, inner, outer_1, inner_1, _og, _ig, _linear, _product,
    outer_grad, inner_grad, linear, product,
):
    scale, bias = scale_ref[0], bias_ref[0]
    even = even_ref[0] == 1
    add_tile(scale, bias, outer, outer_1, outer_grad, linear, product, even)
    add_tile(scale, bias, inner, inner_1, inner_grad, linear, product, jnp.logical_not(even))


def second_tile(even_ref, scale_ref, bias_ref, inner, inner_3, _ig, _linear, _product, inner_grad, linear, product):
    add_tile(scale_ref[0], bias_ref[0], inner, inner_3, inner_grad, linear, product, even_ref[0] == 0)


def passed_tile(
    even_ref, straight_ref, scale_ref, bias_ref, outer, outer_3, _og, _linear, _product, outer_grad, linear, product
):
    @pl.when(straight_ref[0] == 0)
    def _():
        add_tile(scale_ref[0], bias_ref[0], outer, outer_3, outer_grad, linear, product, even_ref[0] == 1)


def last_tiles(
    even_ref, scale_ref, bias_ref, outer, inner, outer_2, inner_2, outer_grad, inner_grad, linear, product,
    out_loss, out_image, out_text, outer_total, inner_total, done,
):
    scale, bias = scale_ref[0], bias_ref[0]
    even = even_ref[0] == 1
    count, width = outer.shape
    tile = width // PARTS

    def results(outer_out, inner_out, has_outer_losses):
        copies = []

        def finish(own, arrived, grad, total, out, has_losses):
            logits = logits_of(own[...], arrived[...], scale, bias)
            small, sigmoid = sigmoid_parts(logits)
            weight = (scale * sigmoid).astype(jnp.bfloat16)
            for i in range(PARTS):
                at = pl.ds(i * tile, tile)
                total[:, at] = grad[:, at] + times(weight, arrived[:, at])
                copies.append(pltpu.make_async_copy(total.at[:, at], out.at[:, at], done.at[len(copies)]))
                copies[-1].start()
            if has_losses:
                sums = linear[...] + jnp.maximum(logits, 0.0) + jnp.log1p(product[...] + small + product[...] * small)
                out_loss[...] = jnp.sum(sums.T, axis=0, keepdims=True) / (STEPS * count)

        finish(inner, inner_2, inner_grad, inner_total, inner_out, not has_outer_losses)
        finish(outer, outer_2, outer_grad, outer_total, outer_out, has_outer_losses)
        for copy in copies:
            copy.wait()

    pl.when(even)(lambda: results(out_image, out_text, True))
    pl.when(jnp.logical_not(even))(lambda: results(out_text, out_image, False))


def call(kernel, ins, outs, shapes, scratch=(), **more):
    return pl.pallas_call(
        kernel,
        out_shape=shapes,
        in_specs=ins,
        out_specs=outs,
        scratch_shapes=list(scratch),
        cost_estimate=pl.CostEstimate(flops=1, bytes_accessed=1, transcendentals=0),
        compiler_params=pltpu.CompilerParams(vmem_limit_bytes=16 * 1024 * 1024),
        **more,
    )


def per_device(picture_encodings, sentence_encodings, sharpness_factor, additive_shift_term):
    count, width = picture_encodings.shape
    place = lax.axis_index(AXES) % 16
    even = jnp.where(place % 2 == 0, 1, 0).astype(jnp.int32).reshape(1)
    is_straight = jnp.where(place == 8, 1, 0).astype(jnp.int32).reshape(1)
    scalars = (sharpness_factor, additive_shift_term)
    grad = jax.ShapeDtypeStruct((count, width), jnp.float32)
    tile = jax.ShapeDtypeStruct((count, count), jnp.float32)

    straight = moved(sentence_encodings, 0, 3, lambda i: i % 16 == 5)
    outer = jnp.where(place % 2 == 0, picture_encodings, sentence_encodings)
    images, texts, outer = lax.optimization_barrier((picture_encodings, sentence_encodings, outer))
    inner = jnp.where(place % 2 == 0, texts, images)
    outer_1 = moved(outer, -1, 1)
    inner_3 = moved(inner, 3, -3)
    inner_1 = moved(inner, 1, -1)
    sums = call(own_tile, [SMEM] * 4 + [VMEM] * 3, [VMEM] * 4, [grad, grad, tile, tile])(
        even, is_straight, *scalars, outer, inner, straight
    )
    outer_1 = after(outer_1, *sums)
    outer_3 = moved(outer_1, 2, -2, lambda i: i % 16 != 6)
    outer_grad, inner_grad, linear, product = call(
        first_tiles, [SMEM] * 3 + [VMEM] * 8, [VMEM] * 4, [grad, grad, tile, tile], input_output_aliases={7: 0, 8: 1, 9: 2, 10: 3}
    )(even, *scalars, outer, inner, outer_1, inner_1, *sums)
    outer_1, inner_3, linear = lax.optimization_barrier((outer_1, inner_3, linear))
    inner_2 = moved(outer_1, 1, -1)
    outer_2 = moved(inner_3, 1, -1)
    inner_grad, linear, product = call(
        second_tile, [SMEM] * 3 + [VMEM] * 5, [VMEM] * 3, [grad, tile, tile], input_output_aliases={5: 0, 6: 1, 7: 2}
    )(even, *scalars, inner, inner_3, inner_grad, linear, product)
    outer_grad, linear, product = call(
        passed_tile, [SMEM] * 4 + [VMEM] * 5, [VMEM] * 3, [grad, tile, tile], input_output_aliases={6: 0, 7: 1, 8: 2}
    )(even, is_straight, *scalars, outer, outer_3, outer_grad, linear, product)
    loss, grad_image, grad_text = call(
        last_tiles,
        [SMEM] * 3 + [VMEM] * 8,
        [VMEM, ANY, ANY],
        [jax.ShapeDtypeStruct((1, count), jnp.float32), grad, grad],
        [pltpu.VMEM((count, width), jnp.float32)] * 2 + [pltpu.SemaphoreType.DMA((2 * PARTS,))],
    )(even, *scalars, outer, inner, outer_2, inner_2, outer_grad, inner_grad, linear, product)
    return loss.reshape(count), grad_image, grad_text


def solution(mesh):
    placed = (P(AXES, None), P(AXES, None), P(), P())
    return jax.shard_map(
        per_device,
        mesh=mesh,
        in_specs=placed,
        out_specs=(P(AXES), P(AXES, None), P(AXES, None)),
        check_vma=False,
    )
```

```python
import jax
import jax.numpy as jnp
from jax import lax
from jax.experimental import pallas as pl
from jax.experimental.pallas import tpu as pltpu
from jax.sharding import PartitionSpec as P

STEPS = 4
AXES = ("blk", "lap")
PARTS = 3
SMEM = pl.BlockSpec(memory_space=pltpu.SMEM)
VMEM = pl.BlockSpec(memory_space=pltpu.VMEM)
ANY = pl.BlockSpec(memory_space=pl.ANY)


def moved(block, even_by, odd_by, sends=lambda i: True):
    count = lax.axis_size(AXES)
    route = [(i, (i + (odd_by if i % 2 else even_by)) % count) for i in range(count) if sends(i)]
    return lax.ppermute(block, AXES, route)


def after(block, *earlier):
    return lax.optimization_barrier((block, *earlier))[0]


def logits_of(own, arrived, scale, bias):
    inner = lax.dot_general(own, arrived, (((1,), (1,)), ((), ())), preferred_element_type=jnp.float32)
    return scale * inner + bias


def sigmoid_parts(logits):
    small = jnp.exp(-jnp.abs(logits))
    return small, jnp.where(logits >= 0.0, 1.0, small) / (1.0 + small)


def times(weight, block):
    return jnp.dot(weight, block, preferred_element_type=jnp.float32)


def add_losses(logits, small, linear, product, counts):
    return linear + counts * jnp.maximum(logits, 0.0), product + counts * (small + product * small)


def weights_of(logits, scale):
    small, sigmoid = sigmoid_parts(logits)
    return small, (scale * sigmoid).astype(jnp.bfloat16)


def parts_of(sums):
    count = sums.shape[0]
    width = (sums.shape[1] - 2 * count) // 2
    starts = (0, width, 2 * width, 2 * width + count)
    return [sums.at[:, pl.ds(start, size)] for start, size in zip(starts, (width, width, count, count), strict=True)]


def add_tile(scale, bias, own, arrived, grad, linear, product, counts):
    logits = logits_of(own[...], arrived[...], scale, bias)
    small, weight = weights_of(logits, scale)
    grad[...] += times(weight, arrived[...])
    linear[...], product[...] = add_losses(logits, small, linear[...], product[...], counts)


def own_tiles(even_ref, straight_ref, scale_ref, bias_ref, outer, inner, straight, sums):
    scale, bias = scale_ref[0], bias_ref[0]
    even = even_ref[0] == 1
    count = outer.shape[0]
    outer_grad, inner_grad, linear, product = parts_of(sums)
    logits = logits_of(outer[...], inner[...], scale, bias)
    matched = lax.broadcasted_iota(jnp.int32, (count, count), 0) == lax.broadcasted_iota(jnp.int32, (count, count), 1)
    sign = jnp.where(matched, -1.0, 1.0)
    logits = sign * logits
    small, sigmoid = sigmoid_parts(logits)
    weight = (scale * sign * sigmoid).astype(jnp.bfloat16)
    outer_grad[...] = times(weight, inner[...])
    inner_grad[...] = lax.dot_general(weight, outer[...], (((0,), (0,)), ((), ())), preferred_element_type=jnp.float32)

    @pl.when(even)
    def _():
        linear[...] = jnp.maximum(logits, 0.0)
        product[...] = small

    @pl.when(jnp.logical_not(even))
    def _():
        linear[...] = jnp.maximum(logits, 0.0).T
        product[...] = small.T

    @pl.when(straight_ref[0] == 1)
    def _():
        add_tile(scale, bias, outer, straight, outer_grad, linear, product, even_ref[0].astype(jnp.float32))


def first_tiles(even_ref, scale_ref, bias_ref, outer, inner, outer_1, inner_1, _sums, sums):
    scale, bias = scale_ref[0], bias_ref[0]
    even = even_ref[0].astype(jnp.float32)
    outer_grad, inner_grad, linear, product = parts_of(sums)
    logits_1 = logits_of(outer[...], outer_1[...], scale, bias)
    logits_2 = logits_of(inner[...], inner_1[...], scale, bias)
    small_1, weight_1 = weights_of(logits_1, scale)
    small_2, weight_2 = weights_of(logits_2, scale)
    outer_grad[...] += times(weight_1, outer_1[...])
    inner_grad[...] += times(weight_2, inner_1[...])
    losses = add_losses(logits_1, small_1, linear[...], product[...], even)
    linear[...], product[...] = add_losses(logits_2, small_2, *losses, 1.0 - even)


def passed_tile(even_ref, straight_ref, scale_ref, bias_ref, outer, outer_3, _sums, sums):
    outer_grad, _, linear, product = parts_of(sums)

    @pl.when(straight_ref[0] == 0)
    def _():
        counts = even_ref[0].astype(jnp.float32)
        add_tile(scale_ref[0], bias_ref[0], outer, outer_3, outer_grad, linear, product, counts)


def inner_tile(even_ref, scale_ref, bias_ref, inner, inner_2, _sums, sums):
    _, inner_grad, linear, product = parts_of(sums)
    counts = 1.0 - even_ref[0].astype(jnp.float32)
    add_tile(scale_ref[0], bias_ref[0], inner, inner_2, inner_grad, linear, product, counts)


def last_tile(even_ref, scale_ref, bias_ref, outer, outer_2, sums, out_loss, out_image, out_text, total, done):
    scale, bias = scale_ref[0], bias_ref[0]
    even = even_ref[0] == 1
    count, width = outer.shape
    tile = width // PARTS
    outer_grad, inner_grad, linear, product = parts_of(sums)

    def results(outer_out, inner_out):
        copies = [pltpu.make_async_copy(inner_grad, inner_out, done.at[PARTS])]
        copies[0].start()
        logits = logits_of(outer[...], outer_2[...], scale, bias)
        small, weight = weights_of(logits, scale)
        for i in range(PARTS):
            at = pl.ds(i * tile, tile)
            total[:, at] = outer_grad[:, at] + times(weight, outer_2[:, at])
            copies.append(pltpu.make_async_copy(total.at[:, at], outer_out.at[:, at], done.at[i]))
            copies[-1].start()
        losses, products = add_losses(logits, small, linear[...], product[...], even_ref[0].astype(jnp.float32))
        out_loss[...] = jnp.sum((losses + jnp.log1p(products)).T, axis=0, keepdims=True) / (STEPS * count)
        for copy in copies:
            copy.wait()

    pl.when(even)(lambda: results(out_image, out_text))
    pl.when(jnp.logical_not(even))(lambda: results(out_text, out_image))


def call(kernel, ins, outs, shapes, scratch=(), flops=1, **more):
    return pl.pallas_call(
        kernel,
        out_shape=shapes,
        in_specs=ins,
        out_specs=outs,
        scratch_shapes=list(scratch),
        cost_estimate=pl.CostEstimate(flops=flops, bytes_accessed=1, transcendentals=0),
        compiler_params=pltpu.CompilerParams(vmem_limit_bytes=16 * 1024 * 1024),
        **more,
    )


def per_device(picture_encodings, sentence_encodings, sharpness_factor, additive_shift_term):
    count, width = picture_encodings.shape
    place = lax.axis_index(AXES) % 16
    even = jnp.where(place % 2 == 0, 1, 0).astype(jnp.int32).reshape(1)
    is_straight = jnp.where(place == 8, 1, 0).astype(jnp.int32).reshape(1)
    scalars = (sharpness_factor, additive_shift_term)
    grad = jax.ShapeDtypeStruct((count, width), jnp.float32)
    state = jax.ShapeDtypeStruct((count, 2 * width + 2 * count), jnp.float32)

    outer = jnp.where(place % 2 == 0, picture_encodings, sentence_encodings)
    images, texts, outer = lax.optimization_barrier((picture_encodings, sentence_encodings, outer))
    inner = jnp.where(place % 2 == 0, texts, images)
    outer_1 = moved(outer, -1, 1)
    straight = moved(sentence_encodings, 0, 3, lambda i: i % 16 == 5)
    inner_3 = moved(inner, 3, -3)
    inner_1 = moved(inner, 1, -1)
    sums = call(own_tiles, [SMEM] * 4 + [VMEM] * 3, VMEM, state)(even, is_straight, *scalars, outer, inner, straight)
    outer_1 = after(outer_1, sums)
    outer_3 = moved(outer_1, 2, -2, lambda i: i % 16 != 6)
    inner_2 = moved(outer_1, 1, -1)
    sums = call(first_tiles, [SMEM] * 3 + [VMEM] * 5, VMEM, state, input_output_aliases={7: 0})(
        even, *scalars, outer, inner, outer_1, inner_1, sums
    )
    inner_3 = after(inner_3, sums)
    outer_2 = moved(inner_3, 1, -1)
    sums = call(inner_tile, [SMEM] * 3 + [VMEM] * 3, VMEM, state, input_output_aliases={5: 0})(
        even, *scalars, inner, inner_3, sums
    )
    sums = call(passed_tile, [SMEM] * 4 + [VMEM] * 3, VMEM, state, input_output_aliases={6: 0})(
        even, is_straight, *scalars, outer, outer_3, sums
    )
    sums = call(inner_tile, [SMEM] * 3 + [VMEM] * 3, VMEM, state, flops=5000000000, input_output_aliases={5: 0})(
        even, *scalars, inner, inner_2, sums
    )
    loss, grad_image, grad_text = call(
        last_tile,
        [SMEM] * 3 + [VMEM] * 3,
        [VMEM, ANY, ANY],
        [jax.ShapeDtypeStruct((1, count), jnp.float32), grad, grad],
        [pltpu.VMEM((count, width), jnp.float32), pltpu.SemaphoreType.DMA((PARTS + 1,))],
    )(even, *scalars, outer, outer_2, sums)
    return loss.reshape(count), grad_image, grad_text


def solution(mesh):
    placed = (P(AXES, None), P(AXES, None), P(), P())
    return jax.shard_map(
        per_device,
        mesh=mesh,
        in_specs=placed,
        out_specs=(P(AXES), P(AXES, None), P(AXES, None)),
        check_vma=False,
    )
```

```python
import jax
import jax.numpy as jnp
from jax import lax
from jax.experimental import pallas as pl
from jax.experimental.pallas import tpu as pltpu
from jax.sharding import PartitionSpec as P

STEPS = 4
AXES = ("blk", "lap")
PARTS = 3
SMEM = pl.BlockSpec(memory_space=pltpu.SMEM)
VMEM = pl.BlockSpec(memory_space=pltpu.VMEM)
ANY = pl.BlockSpec(memory_space=pl.ANY)


def moved(block, even_by, odd_by, sends=lambda i: True):
    count = lax.axis_size(AXES)
    route = [(i, (i + (odd_by if i % 2 else even_by)) % count) for i in range(count) if sends(i)]
    return lax.ppermute(block, AXES, route)


def after(block, *earlier):
    return lax.optimization_barrier((block, *earlier))[0]


def logits_of(own, arrived, scale, bias):
    inner = lax.dot_general(own, arrived, (((1,), (1,)), ((), ())), preferred_element_type=jnp.float32)
    return scale * inner + bias


def sigmoid_parts(logits):
    small = jnp.exp(-jnp.abs(logits))
    return small, jnp.where(logits >= 0.0, 1.0, small) / (1.0 + small)


def times(weight, block):
    return jnp.dot(weight, block, preferred_element_type=jnp.float32)


def add_losses(logits, small, linear, product, counts):
    return linear + counts * jnp.maximum(logits, 0.0), product + counts * (small + product * small)


def weights_of(logits, scale):
    small, sigmoid = sigmoid_parts(logits)
    return small, (scale * sigmoid).astype(jnp.bfloat16)


def parts_of(sums):
    count = sums.shape[0]
    width = (sums.shape[1] - 2 * count) // 2
    starts = (0, width, 2 * width, 2 * width + count)
    return [sums.at[:, pl.ds(start, size)] for start, size in zip(starts, (width, width, count, count), strict=True)]


def add_tile(scale, bias, own, arrived, grad, linear, product, counts):
    logits = logits_of(own[...], arrived[...], scale, bias)
    small, weight = weights_of(logits, scale)
    grad[...] += times(weight, arrived[...])
    linear[...], product[...] = add_losses(logits, small, linear[...], product[...], counts)


def own_tiles(even_ref, straight_ref, scale_ref, bias_ref, outer, inner, straight, sums):
    scale, bias = scale_ref[0], bias_ref[0]
    even = even_ref[0] == 1
    count = outer.shape[0]
    outer_grad, inner_grad, linear, product = parts_of(sums)
    logits = logits_of(outer[...], inner[...], scale, bias)
    matched = lax.broadcasted_iota(jnp.int32, (count, count), 0) == lax.broadcasted_iota(jnp.int32, (count, count), 1)
    sign = jnp.where(matched, -1.0, 1.0)
    logits = sign * logits
    small, sigmoid = sigmoid_parts(logits)
    weight = (scale * sign * sigmoid).astype(jnp.bfloat16)
    outer_grad[...] = times(weight, inner[...])
    inner_grad[...] = lax.dot_general(weight, outer[...], (((0,), (0,)), ((), ())), preferred_element_type=jnp.float32)

    @pl.when(even)
    def _():
        linear[...] = jnp.maximum(logits, 0.0)
        product[...] = small

    @pl.when(jnp.logical_not(even))
    def _():
        linear[...] = jnp.maximum(logits, 0.0).T
        product[...] = small.T

    @pl.when(straight_ref[0] == 1)
    def _():
        add_tile(scale, bias, outer, straight, outer_grad, linear, product, even_ref[0].astype(jnp.float32))


def first_tiles(even_ref, scale_ref, bias_ref, outer, inner, outer_1, inner_1, inner_2a, inner_2b, _sums, sums):
    scale, bias = scale_ref[0], bias_ref[0]
    even = even_ref[0].astype(jnp.float32)
    half = inner_2a.shape[0]
    outer_grad, inner_grad, linear, product = parts_of(sums)
    logits_1 = logits_of(outer[...], outer_1[...], scale, bias)
    logits_2 = logits_of(inner[...], inner_1[...], scale, bias)
    logits_a = logits_of(inner[...], inner_2a[...], scale, bias)
    logits_b = logits_of(inner[...], inner_2b[...], scale, bias)
    small_1, weight_1 = weights_of(logits_1, scale)
    small_2, weight_2 = weights_of(logits_2, scale)
    small_a, weight_a = weights_of(logits_a, scale)
    small_b, weight_b = weights_of(logits_b, scale)
    outer_grad[...] += times(weight_1, outer_1[...])
    inner_grad[...] += times(weight_2, inner_1[...]) + times(weight_a, inner_2a[...]) + times(weight_b, inner_2b[...])
    losses = add_losses(logits_1, small_1, linear[...], product[...], even)
    linear[...], product[...] = add_losses(logits_2, small_2, *losses, 1.0 - even)
    for i, (logits, small) in enumerate(((logits_a, small_a), (logits_b, small_b))):
        at = pl.ds(i * half, half)
        linear[:, at], product[:, at] = add_losses(logits, small, linear[:, at], product[:, at], 1.0 - even)


def second_tiles(even_ref, straight_ref, scale_ref, bias_ref, outer, inner, outer_3, inner_3, _sums, sums):
    scale, bias = scale_ref[0], bias_ref[0]
    even = even_ref[0].astype(jnp.float32)
    passed = 1.0 - straight_ref[0].astype(jnp.float32)
    outer_grad, inner_grad, linear, product = parts_of(sums)
    inner_logits = logits_of(inner[...], inner_3[...], scale, bias)
    outer_logits = logits_of(outer[...], outer_3[...], scale, bias)
    inner_small, inner_weight = weights_of(inner_logits, scale)
    outer_small, outer_weight = weights_of(outer_logits, scale)
    inner_grad[...] += times(inner_weight, inner_3[...])
    outer_grad[...] += times(outer_weight, outer_3[...])
    losses = add_losses(inner_logits, inner_small, linear[...], product[...], 1.0 - even)
    linear[...], product[...] = add_losses(outer_logits, outer_small, *losses, even * passed)


def last_tile(even_ref, scale_ref, bias_ref, outer, outer_2, sums, out_loss, out_image, out_text, total, done):
    scale, bias = scale_ref[0], bias_ref[0]
    even = even_ref[0] == 1
    count, width = outer.shape
    tile = width // PARTS
    outer_grad, inner_grad, linear, product = parts_of(sums)

    def results(outer_out, inner_out):
        copies = [pltpu.make_async_copy(inner_grad, inner_out, done.at[PARTS])]
        copies[0].start()
        logits = logits_of(outer[...], outer_2[...], scale, bias)
        small, weight = weights_of(logits, scale)
        for i in range(PARTS):
            at = pl.ds(i * tile, tile)
            total[:, at] = outer_grad[:, at] + times(weight, outer_2[:, at])
            copies.append(pltpu.make_async_copy(total.at[:, at], outer_out.at[:, at], done.at[i]))
            copies[-1].start()
        losses, products = add_losses(logits, small, linear[...], product[...], even_ref[0].astype(jnp.float32))
        out_loss[...] = jnp.sum((losses + jnp.log1p(products)).T, axis=0, keepdims=True) / (STEPS * count)
        for copy in copies:
            copy.wait()

    pl.when(even)(lambda: results(out_image, out_text))
    pl.when(jnp.logical_not(even))(lambda: results(out_text, out_image))


def call(kernel, ins, outs, shapes, scratch=(), flops=1, **more):
    return pl.pallas_call(
        kernel,
        out_shape=shapes,
        in_specs=ins,
        out_specs=outs,
        scratch_shapes=list(scratch),
        cost_estimate=pl.CostEstimate(flops=flops, bytes_accessed=1, transcendentals=0),
        compiler_params=pltpu.CompilerParams(vmem_limit_bytes=16 * 1024 * 1024),
        **more,
    )


def per_device(picture_encodings, sentence_encodings, sharpness_factor, additive_shift_term):
    count, width = picture_encodings.shape
    place = lax.axis_index(AXES) % 16
    even = jnp.where(place % 2 == 0, 1, 0).astype(jnp.int32).reshape(1)
    is_straight = jnp.where(place == 8, 1, 0).astype(jnp.int32).reshape(1)
    scalars = (sharpness_factor, additive_shift_term)
    grad = jax.ShapeDtypeStruct((count, width), jnp.float32)
    state = jax.ShapeDtypeStruct((count, 2 * width + 2 * count), jnp.float32)

    outer = jnp.where(place % 2 == 0, picture_encodings, sentence_encodings)
    images, texts, outer = lax.optimization_barrier((picture_encodings, sentence_encodings, outer))
    inner = jnp.where(place % 2 == 0, texts, images)
    outer_1 = moved(outer, -1, 1)
    straight = moved(sentence_encodings, 0, 3, lambda i: i % 16 == 5)
    inner_3 = moved(inner, 3, -3)
    inner_1 = moved(inner, 1, -1)
    sums = call(own_tiles, [SMEM] * 4 + [VMEM] * 3, VMEM, state)(even, is_straight, *scalars, outer, inner, straight)
    outer_1 = after(outer_1, sums)
    outer_3 = moved(outer_1, 2, -2, lambda i: i % 16 != 6)
    inner_2 = [moved(part, 1, -1) for part in (outer_1[: count // 2], outer_1[count // 2 :])]
    sums = call(first_tiles, [SMEM] * 3 + [VMEM] * 7, VMEM, state, input_output_aliases={9: 0})(
        even, *scalars, outer, inner, outer_1, inner_1, *inner_2, sums
    )
    inner_3 = after(inner_3, sums)
    outer_2 = moved(inner_3, 1, -1)
    sums = call(second_tiles, [SMEM] * 4 + [VMEM] * 5, VMEM, state, flops=20000000000, input_output_aliases={8: 0})(
        even, is_straight, *scalars, outer, inner, outer_3, inner_3, sums
    )
    loss, grad_image, grad_text = call(
        last_tile,
        [SMEM] * 3 + [VMEM] * 3,
        [VMEM, ANY, ANY],
        [jax.ShapeDtypeStruct((1, count), jnp.float32), grad, grad],
        [pltpu.VMEM((count, width), jnp.float32), pltpu.SemaphoreType.DMA((PARTS + 1,))],
    )(even, *scalars, outer, outer_2, sums)
    return loss.reshape(count), grad_image, grad_text


def solution(mesh):
    placed = (P(AXES, None), P(AXES, None), P(), P())
    return jax.shard_map(
        per_device,
        mesh=mesh,
        in_specs=placed,
        out_specs=(P(AXES), P(AXES, None), P(AXES, None)),
        check_vma=False,
    )
```

```python
import jax
import jax.numpy as jnp
from jax import lax
from jax.experimental import pallas as pl
from jax.experimental.pallas import tpu as pltpu
from jax.sharding import PartitionSpec as P

STEPS = 4
AXES = ("blk", "lap")
PARTS = 3
SMEM = pl.BlockSpec(memory_space=pltpu.SMEM)
VMEM = pl.BlockSpec(memory_space=pltpu.VMEM)
ANY = pl.BlockSpec(memory_space=pl.ANY)


def moved(block, even_by, odd_by, sends=lambda i: True):
    count = lax.axis_size(AXES)
    route = [(i, (i + (odd_by if i % 2 else even_by)) % count) for i in range(count) if sends(i)]
    return lax.ppermute(block, AXES, route)


def after(block, *earlier):
    return lax.optimization_barrier((block, *earlier))[0]


def logits_of(own, arrived, scale, bias):
    inner = lax.dot_general(own, arrived, (((1,), (1,)), ((), ())), preferred_element_type=jnp.float32)
    return scale * inner + bias


def sigmoid_parts(logits):
    small = jnp.exp(-jnp.abs(logits))
    return small, jnp.where(logits >= 0.0, 1.0, small) / (1.0 + small)


def times(weight, block):
    return jnp.dot(weight, block, preferred_element_type=jnp.float32)


def add_losses(logits, small, linear, product, counts):
    return linear + counts * jnp.maximum(logits, 0.0), product + counts * (small + product * small)


def weights_of(logits, scale):
    small, sigmoid = sigmoid_parts(logits)
    return small, (scale * sigmoid).astype(jnp.bfloat16)


def parts_of(sums):
    count = sums.shape[0]
    width = (sums.shape[1] - 2 * count) // 2
    starts = (0, width, 2 * width, 2 * width + count)
    return [sums.at[:, pl.ds(start, size)] for start, size in zip(starts, (width, width, count, count), strict=True)]


def add_tile(scale, bias, own, arrived, grad, linear, product, counts):
    logits = logits_of(own[...], arrived[...], scale, bias)
    small, weight = weights_of(logits, scale)
    grad[...] += times(weight, arrived[...])
    linear[...], product[...] = add_losses(logits, small, linear[...], product[...], counts)


def own_tiles(even_ref, straight_ref, scale_ref, bias_ref, outer, inner, straight, sums):
    scale, bias = scale_ref[0], bias_ref[0]
    even = even_ref[0] == 1
    count = outer.shape[0]
    outer_grad, inner_grad, linear, product = parts_of(sums)
    logits = logits_of(outer[...], inner[...], scale, bias)
    matched = lax.broadcasted_iota(jnp.int32, (count, count), 0) == lax.broadcasted_iota(jnp.int32, (count, count), 1)
    sign = jnp.where(matched, -1.0, 1.0)
    logits = sign * logits
    small, sigmoid = sigmoid_parts(logits)
    weight = (scale * sign * sigmoid).astype(jnp.bfloat16)
    outer_grad[...] = times(weight, inner[...])
    inner_grad[...] = lax.dot_general(weight, outer[...], (((0,), (0,)), ((), ())), preferred_element_type=jnp.float32)

    @pl.when(even)
    def _():
        linear[...] = jnp.maximum(logits, 0.0)
        product[...] = small

    @pl.when(jnp.logical_not(even))
    def _():
        linear[...] = jnp.maximum(logits, 0.0).T
        product[...] = small.T

    @pl.when(straight_ref[0] == 1)
    def _():
        add_tile(scale, bias, outer, straight, outer_grad, linear, product, even_ref[0].astype(jnp.float32))


def first_tiles(even_ref, scale_ref, bias_ref, outer, inner, outer_1, inner_1, inner_2a, inner_2b, _sums, sums):
    scale, bias = scale_ref[0], bias_ref[0]
    even = even_ref[0].astype(jnp.float32)
    half = inner_2a.shape[0]
    outer_grad, inner_grad, linear, product = parts_of(sums)
    logits_1 = logits_of(outer[...], outer_1[...], scale, bias)
    logits_2 = logits_of(inner[...], inner_1[...], scale, bias)
    logits_a = logits_of(inner[...], inner_2a[...], scale, bias)
    logits_b = logits_of(inner[...], inner_2b[...], scale, bias)
    small_1, weight_1 = weights_of(logits_1, scale)
    small_2, weight_2 = weights_of(logits_2, scale)
    small_a, weight_a = weights_of(logits_a, scale)
    small_b, weight_b = weights_of(logits_b, scale)
    outer_grad[...] += times(weight_1, outer_1[...])
    inner_grad[...] += times(weight_2, inner_1[...]) + times(weight_a, inner_2a[...]) + times(weight_b, inner_2b[...])
    losses = add_losses(logits_1, small_1, linear[...], product[...], even)
    linear[...], product[...] = add_losses(logits_2, small_2, *losses, 1.0 - even)
    for i, (logits, small) in enumerate(((logits_a, small_a), (logits_b, small_b))):
        at = pl.ds(i * half, half)
        linear[:, at], product[:, at] = add_losses(logits, small, linear[:, at], product[:, at], 1.0 - even)


def second_tiles(even_ref, straight_ref, scale_ref, bias_ref, outer, inner, outer_3, inner_3, _sums, sums, weight_3):
    scale, bias = scale_ref[0], bias_ref[0]
    even = even_ref[0].astype(jnp.float32)
    passed = 1.0 - straight_ref[0].astype(jnp.float32)
    _, inner_grad, linear, product = parts_of(sums)
    inner_logits = logits_of(inner[...], inner_3[...], scale, bias)
    outer_logits = logits_of(outer[...], outer_3[...], scale, bias)
    inner_small, inner_weight = weights_of(inner_logits, scale)
    outer_small, outer_weight = weights_of(outer_logits, scale)
    inner_grad[...] += times(inner_weight, inner_3[...])
    weight_3[...] = outer_weight
    losses = add_losses(inner_logits, inner_small, linear[...], product[...], 1.0 - even)
    linear[...], product[...] = add_losses(outer_logits, outer_small, *losses, even * passed)


def last_tile(even_ref, scale_ref, bias_ref, outer, outer_2, outer_3, weight_3, sums, out_loss, out_image, out_text, total, done):
    scale, bias = scale_ref[0], bias_ref[0]
    even = even_ref[0] == 1
    count, width = outer.shape
    tile = width // PARTS
    outer_grad, inner_grad, linear, product = parts_of(sums)

    def results(outer_out, inner_out):
        copies = [pltpu.make_async_copy(inner_grad, inner_out, done.at[PARTS])]
        copies[0].start()
        logits = logits_of(outer[...], outer_2[...], scale, bias)
        small, weight = weights_of(logits, scale)
        for i in range(PARTS):
            at = pl.ds(i * tile, tile)
            total[:, at] = outer_grad[:, at] + times(weight_3[...], outer_3[:, at]) + times(weight, outer_2[:, at])
            copies.append(pltpu.make_async_copy(total.at[:, at], outer_out.at[:, at], done.at[i]))
            copies[-1].start()
        losses, products = add_losses(logits, small, linear[...], product[...], even_ref[0].astype(jnp.float32))
        out_loss[...] = jnp.sum((losses + jnp.log1p(products)).T, axis=0, keepdims=True) / (STEPS * count)
        for copy in copies:
            copy.wait()

    pl.when(even)(lambda: results(out_image, out_text))
    pl.when(jnp.logical_not(even))(lambda: results(out_text, out_image))


def call(kernel, ins, outs, shapes, scratch=(), flops=1, **more):
    return pl.pallas_call(
        kernel,
        out_shape=shapes,
        in_specs=ins,
        out_specs=outs,
        scratch_shapes=list(scratch),
        cost_estimate=pl.CostEstimate(flops=flops, bytes_accessed=1, transcendentals=0),
        compiler_params=pltpu.CompilerParams(vmem_limit_bytes=16 * 1024 * 1024),
        **more,
    )


def per_device(picture_encodings, sentence_encodings, sharpness_factor, additive_shift_term):
    count, width = picture_encodings.shape
    place = lax.axis_index(AXES) % 16
    even = jnp.where(place % 2 == 0, 1, 0).astype(jnp.int32).reshape(1)
    is_straight = jnp.where(place == 8, 1, 0).astype(jnp.int32).reshape(1)
    scalars = (sharpness_factor, additive_shift_term)
    grad = jax.ShapeDtypeStruct((count, width), jnp.float32)
    state = jax.ShapeDtypeStruct((count, 2 * width + 2 * count), jnp.float32)

    outer = jnp.where(place % 2 == 0, picture_encodings, sentence_encodings)
    images, texts, outer = lax.optimization_barrier((picture_encodings, sentence_encodings, outer))
    inner = jnp.where(place % 2 == 0, texts, images)
    outer_1 = moved(outer, -1, 1)
    straight = moved(sentence_encodings, 0, 3, lambda i: i % 16 == 5)
    inner_3 = moved(inner, 3, -3)
    inner_1 = moved(inner, 1, -1)
    sums = call(own_tiles, [SMEM] * 4 + [VMEM] * 3, VMEM, state)(even, is_straight, *scalars, outer, inner, straight)
    outer_1 = after(outer_1, sums)
    outer_3 = moved(outer_1, 2, -2, lambda i: i % 16 != 6)
    inner_2 = [moved(part, 1, -1) for part in (outer_1[: count // 2], outer_1[count // 2 :])]
    sums = call(first_tiles, [SMEM] * 3 + [VMEM] * 7, VMEM, state, input_output_aliases={9: 0})(
        even, *scalars, outer, inner, outer_1, inner_1, *inner_2, sums
    )
    inner_3 = after(inner_3, sums)
    outer_2 = moved(inner_3, 1, -1)
    weight = jax.ShapeDtypeStruct((count, count), jnp.bfloat16)
    sums, weight_3 = call(second_tiles, [SMEM] * 4 + [VMEM] * 5, [VMEM] * 2, [state, weight], flops=20000000000, input_output_aliases={8: 0})(
        even, is_straight, *scalars, outer, inner, outer_3, inner_3, sums
    )
    loss, grad_image, grad_text = call(
        last_tile,
        [SMEM] * 3 + [VMEM] * 5,
        [VMEM, ANY, ANY],
        [jax.ShapeDtypeStruct((1, count), jnp.float32), grad, grad],
        [pltpu.VMEM((count, width), jnp.float32), pltpu.SemaphoreType.DMA((PARTS + 1,))],
    )(even, *scalars, outer, outer_2, outer_3, weight_3, sums)
    return loss.reshape(count), grad_image, grad_text


def solution(mesh):
    placed = (P(AXES, None), P(AXES, None), P(), P())
    return jax.shard_map(
        per_device,
        mesh=mesh,
        in_specs=placed,
        out_specs=(P(AXES), P(AXES, None), P(AXES, None)),
        check_vma=False,
    )
```

```python
import jax
import jax.numpy as jnp
from jax import lax
from jax.experimental import pallas as pl
from jax.experimental.pallas import tpu as pltpu
from jax.sharding import PartitionSpec as P

STEPS = 4
AXES = ("blk", "lap")
PARTS = 3
SMEM = pl.BlockSpec(memory_space=pltpu.SMEM)
VMEM = pl.BlockSpec(memory_space=pltpu.VMEM)
ANY = pl.BlockSpec(memory_space=pl.ANY)


def moved(block, even_by, odd_by, sends=lambda i: True):
    count = lax.axis_size(AXES)
    route = [(i, (i + (odd_by if i % 2 else even_by)) % count) for i in range(count) if sends(i)]
    return lax.ppermute(block, AXES, route)


def after(block, *earlier):
    return lax.optimization_barrier((block, *earlier))[0]


def logits_of(own, arrived, scale, bias):
    inner = lax.dot_general(own, arrived, (((1,), (1,)), ((), ())), preferred_element_type=jnp.float32)
    return scale * inner + bias


def sigmoid_parts(logits):
    small = jnp.exp(-jnp.abs(logits))
    return small, jnp.where(logits >= 0.0, 1.0, small) / (1.0 + small)


def times(weight, block):
    return jnp.dot(weight, block, preferred_element_type=jnp.float32)


def add_losses(logits, small, linear, product, counts):
    return linear + counts * jnp.maximum(logits, 0.0), product + counts * (small + product * small)


def weights_of(logits, scale):
    small, sigmoid = sigmoid_parts(logits)
    return small, (scale * sigmoid).astype(jnp.bfloat16)


def parts_of(sums):
    count = sums.shape[0]
    width = (sums.shape[1] - 2 * count) // 2
    starts = (0, width, 2 * width, 2 * width + count)
    return [sums.at[:, pl.ds(start, size)] for start, size in zip(starts, (width, width, count, count), strict=True)]


def add_tile(scale, bias, own, arrived, grad, linear, product, counts):
    logits = logits_of(own[...], arrived[...], scale, bias)
    small, weight = weights_of(logits, scale)
    grad[...] += times(weight, arrived[...])
    linear[...], product[...] = add_losses(logits, small, linear[...], product[...], counts)


def own_tiles(even_ref, straight_ref, scale_ref, bias_ref, outer, inner, straight, sums):
    scale, bias = scale_ref[0], bias_ref[0]
    even = even_ref[0] == 1
    count = outer.shape[0]
    outer_grad, inner_grad, linear, product = parts_of(sums)
    logits = logits_of(outer[...], inner[...], scale, bias)
    matched = lax.broadcasted_iota(jnp.int32, (count, count), 0) == lax.broadcasted_iota(jnp.int32, (count, count), 1)
    sign = jnp.where(matched, -1.0, 1.0)
    logits = sign * logits
    small, sigmoid = sigmoid_parts(logits)
    weight = (scale * sign * sigmoid).astype(jnp.bfloat16)
    outer_grad[...] = times(weight, inner[...])
    inner_grad[...] = lax.dot_general(weight, outer[...], (((0,), (0,)), ((), ())), preferred_element_type=jnp.float32)

    @pl.when(even)
    def _():
        linear[...] = jnp.maximum(logits, 0.0)
        product[...] = small

    @pl.when(jnp.logical_not(even))
    def _():
        linear[...] = jnp.maximum(logits, 0.0).T
        product[...] = small.T

    @pl.when(straight_ref[0] == 1)
    def _():
        add_tile(scale, bias, outer, straight, outer_grad, linear, product, even_ref[0].astype(jnp.float32))


def first_tiles(even_ref, scale_ref, bias_ref, outer, inner, outer_1, inner_1, inner_2a, inner_2b, _sums, sums):
    scale, bias = scale_ref[0], bias_ref[0]
    even = even_ref[0].astype(jnp.float32)
    half = inner_2a.shape[0]
    outer_grad, inner_grad, linear, product = parts_of(sums)
    logits_1 = logits_of(outer[...], outer_1[...], scale, bias)
    logits_2 = logits_of(inner[...], inner_1[...], scale, bias)
    logits_a = logits_of(inner[...], inner_2a[...], scale, bias)
    logits_b = logits_of(inner[...], inner_2b[...], scale, bias)
    small_1, weight_1 = weights_of(logits_1, scale)
    small_2, weight_2 = weights_of(logits_2, scale)
    small_a, weight_a = weights_of(logits_a, scale)
    small_b, weight_b = weights_of(logits_b, scale)
    outer_grad[...] += times(weight_1, outer_1[...])
    inner_grad[...] += times(weight_2, inner_1[...]) + times(weight_a, inner_2a[...]) + times(weight_b, inner_2b[...])
    losses = add_losses(logits_1, small_1, linear[...], product[...], even)
    linear[...], product[...] = add_losses(logits_2, small_2, *losses, 1.0 - even)
    for i, (logits, small) in enumerate(((logits_a, small_a), (logits_b, small_b))):
        at = pl.ds(i * half, half)
        linear[:, at], product[:, at] = add_losses(logits, small, linear[:, at], product[:, at], 1.0 - even)


def second_tiles(even_ref, straight_ref, scale_ref, bias_ref, outer, inner, outer_3, inner_3, _sums, sums, weight_3):
    scale, bias = scale_ref[0], bias_ref[0]
    even = even_ref[0].astype(jnp.float32)
    passed = 1.0 - straight_ref[0].astype(jnp.float32)
    _, inner_grad, linear, product = parts_of(sums)
    inner_logits = logits_of(inner[...], inner_3[...], scale, bias)
    outer_logits = logits_of(outer[...], outer_3[...], scale, bias)
    inner_small, inner_weight = weights_of(inner_logits, scale)
    outer_small, outer_weight = weights_of(outer_logits, scale)
    inner_grad[...] += times(inner_weight, inner_3[...])
    weight_3[...] = outer_weight
    losses = add_losses(inner_logits, inner_small, linear[...], product[...], 1.0 - even)
    linear[...], product[...] = add_losses(outer_logits, outer_small, *losses, even * passed)


def last_tile(even_ref, scale_ref, bias_ref, outer, outer_2, outer_3, weight_3, sums, out_loss, out_image, out_text, total, done):
    scale, bias = scale_ref[0], bias_ref[0]
    even = even_ref[0] == 1
    count, width = outer.shape
    tile = width // PARTS
    outer_grad, inner_grad, linear, product = parts_of(sums)

    def results(outer_out, inner_out):
        copies = []
        for i in range(PARTS):
            at = pl.ds(i * tile, tile)
            copies.append(pltpu.make_async_copy(inner_grad.at[:, at], inner_out.at[:, at], done.at[PARTS + i]))
            copies[-1].start()
        logits = logits_of(outer[...], outer_2[...], scale, bias)
        small, weight = weights_of(logits, scale)
        for i in range(PARTS):
            at = pl.ds(i * tile, tile)
            total[:, at] = outer_grad[:, at] + times(weight_3[...], outer_3[:, at]) + times(weight, outer_2[:, at])
            copies.append(pltpu.make_async_copy(total.at[:, at], outer_out.at[:, at], done.at[i]))
            copies[-1].start()
        losses, products = add_losses(logits, small, linear[...], product[...], even_ref[0].astype(jnp.float32))
        out_loss[...] = jnp.sum((losses + jnp.log1p(products)).T, axis=0, keepdims=True) / (STEPS * count)
        for copy in copies:
            copy.wait()

    pl.when(even)(lambda: results(out_image, out_text))
    pl.when(jnp.logical_not(even))(lambda: results(out_text, out_image))


def call(kernel, ins, outs, shapes, scratch=(), flops=1, **more):
    return pl.pallas_call(
        kernel,
        out_shape=shapes,
        in_specs=ins,
        out_specs=outs,
        scratch_shapes=list(scratch),
        cost_estimate=pl.CostEstimate(flops=flops, bytes_accessed=1, transcendentals=0),
        compiler_params=pltpu.CompilerParams(vmem_limit_bytes=16 * 1024 * 1024),
        **more,
    )


def per_device(picture_encodings, sentence_encodings, sharpness_factor, additive_shift_term):
    count, width = picture_encodings.shape
    place = lax.axis_index(AXES) % 16
    even = jnp.where(place % 2 == 0, 1, 0).astype(jnp.int32).reshape(1)
    is_straight = jnp.where(place == 8, 1, 0).astype(jnp.int32).reshape(1)
    scalars = (sharpness_factor, additive_shift_term)
    grad = jax.ShapeDtypeStruct((count, width), jnp.float32)
    state = jax.ShapeDtypeStruct((count, 2 * width + 2 * count), jnp.float32)

    outer = jnp.where(place % 2 == 0, picture_encodings, sentence_encodings)
    images, texts, outer = lax.optimization_barrier((picture_encodings, sentence_encodings, outer))
    inner = jnp.where(place % 2 == 0, texts, images)
    outer_1 = moved(outer, -1, 1)
    straight = moved(sentence_encodings, 0, 3, lambda i: i % 16 == 5)
    inner_3 = moved(inner, 3, -3)
    inner_1 = moved(inner, 1, -1)
    sums = call(own_tiles, [SMEM] * 4 + [VMEM] * 3, VMEM, state)(even, is_straight, *scalars, outer, inner, straight)
    outer_1 = after(outer_1, sums)
    outer_3 = moved(outer_1, 2, -2, lambda i: i % 16 != 6)
    inner_2 = [moved(part, 1, -1) for part in (outer_1[: count // 2], outer_1[count // 2 :])]
    sums = call(first_tiles, [SMEM] * 3 + [VMEM] * 7, VMEM, state, input_output_aliases={9: 0})(
        even, *scalars, outer, inner, outer_1, inner_1, *inner_2, sums
    )
    inner_3 = after(inner_3, sums)
    outer_2 = moved(inner_3, 1, -1)
    weight = jax.ShapeDtypeStruct((count, count), jnp.bfloat16)
    sums, weight_3 = call(second_tiles, [SMEM] * 4 + [VMEM] * 5, [VMEM] * 2, [state, weight], flops=20000000000, input_output_aliases={8: 0})(
        even, is_straight, *scalars, outer, inner, outer_3, inner_3, sums
    )
    loss, grad_image, grad_text = call(
        last_tile,
        [SMEM] * 3 + [VMEM] * 5,
        [VMEM, ANY, ANY],
        [jax.ShapeDtypeStruct((1, count), jnp.float32), grad, grad],
        [pltpu.VMEM((count, width), jnp.float32), pltpu.SemaphoreType.DMA((2 * PARTS,))],
    )(even, *scalars, outer, outer_2, outer_3, weight_3, sums)
    return loss.reshape(count), grad_image, grad_text


def solution(mesh):
    placed = (P(AXES, None), P(AXES, None), P(), P())
    return jax.shard_map(
        per_device,
        mesh=mesh,
        in_specs=placed,
        out_specs=(P(AXES), P(AXES, None), P(AXES, None)),
        check_vma=False,
    )
```
